128 devices in a mesh: sec: 8 (over x, core), op: 16 (over y, z).
Axes of the slice: x: 4, y: 4, z: 4, core: 2. Of those that a mesh axis runs over, the one named last changes fastest.
Arguments:
- psi: bfloat16 [8192, 256], P(('sec', 'op')), may hold values from -6 to 6
- left_env: bfloat16 [384, 32, 256, 256], P('op', 'sec'), may hold values from -0.01953125 to 0.01953125
- right_env: bfloat16 [384, 32, 256, 256], P('op', 'sec'), may hold values from -0.375 to 0.375
- term_src: int32 [384, 32], P('op', 'sec'), may hold values from 0 to 31, as said below
- block_dims: int32 [2, 32], replicated, may hold values from 64 to 256, as said below
Outputs:
- sigma: bfloat16 [8192, 256], P(('sec', 'op'))
The draws below stay inside these ranges and needn't reach their ends.
Inputs may be any that keep to these rules, and one draw needn't show every extreme that they name: |term_src[t, k] - k| <= 2 for every t and k, and term_src[t, k] = k + 2 for some t and k. `block_dims`: every entry is a multiple of 4; 256 is reached in each row.
All inputs are finite; a program needn't handle non-finite values.
Results may differ from the reference program's by a relative error of at most 0.0049.
Values may be sent and summed in bfloat16 or wider, within the bound.
A program may use at most 128 MiB of HBM per device.

```python
import jax
import jax.numpy as jnp
from jax import lax

BLK = 64
DLOC = 4
W = 256
REACH = 2
NBLK = 32
TERMS = 384


def draw_term_src(key, part):
    delta = jax.random.randint(key, (TERMS, NBLK), -REACH, REACH + 1)
    base = jnp.arange(NBLK, dtype=jnp.int32)[None, :]
    source = jnp.clip(base + delta, 0, NBLK - 1)
    picked = jax.random.randint(jax.random.fold_in(key, 1), (), 0, TERMS)
    middle = NBLK // 2
    source = source.at[picked, middle].set(middle + REACH)
    return source.astype(jnp.int32)


def draw_block_dims(key, part):
    units = jax.random.randint(key, (2, NBLK), BLK // 4, BLK + 1)
    dims = DLOC * units
    chosen = jax.random.randint(jax.random.fold_in(key, 2), (2,), 0, NBLK)
    column = jnp.arange(NBLK, dtype=jnp.int32)[None, :]
    dims = jnp.where(column == chosen[:, None], W, dims)
    return dims.astype(jnp.int32)


def block_scale(rng, shape, shards, low, largest):
    gain, own = 1.0, jax.random.fold_in(rng, 6)
    for position, parts in shards:
        heights = jnp.exp(jax.random.uniform(jax.random.fold_in(own, position), (parts,), jnp.float32, low / len(shards), largest / len(shards)))
        gain = gain * jnp.repeat(heights, shape[position] // parts).reshape([-1 if axis == position else 1 for axis in range(len(shape))])
    return gain


def gaussian(key, extent, scale, limit, shards=(), held_as=jnp.bfloat16):
    array = jax.random.normal(key, extent, jnp.float32) * scale
    if len(shards) > 0:
        array = block_scale(key, extent, shards, -0.22, 0.18) * array
    return jnp.clip(array, min=-limit, max=limit).astype(held_as)


def setup_inputs(seed: int = 0) -> dict:
    arg_keys = jax.random.split(jax.random.key(seed), 6)
    psi = gaussian(arg_keys[0], (NBLK * W, W), 1.0, 6.0, ((0, 128),))
    left_env = gaussian(arg_keys[1], (TERMS, NBLK, W, W), (W * TERMS) ** -0.5, 0.01953125, ((0, 16), (1, 8)))
    right_env = gaussian(arg_keys[2], (TERMS, NBLK, W, W), W ** -0.5, 0.375, ((0, 16), (1, 8)))
    term_src = draw_term_src(jax.random.fold_in(arg_keys[5], 71), 0)
    block_dims = draw_block_dims(jax.random.fold_in(arg_keys[5], 71), 0)
    return {"psi": psi, "left_env": left_env, "right_env": right_env, "term_src": term_src, "block_dims": block_dims}


def reference(psi, left_env, right_env, term_src, block_dims):
    blocks = psi.reshape(NBLK, W, W)
    places = jnp.arange(W, dtype=jnp.int32)
    row_ok = places[None, :] < block_dims[0][:, None]
    col_ok = places[None, :] < block_dims[1][:, None]
    keep = row_ok[:, :, None] & col_ok[:, None, :]
    masked = jnp.where(keep, blocks, jnp.zeros_like(blocks)).astype(jnp.bfloat16)

    def per_block(block_id):
        def per_term(running, term_id):
            source = masked[term_src[term_id, block_id]]
            half = jnp.dot(source, right_env[term_id, block_id], preferred_element_type=jnp.float32).astype(jnp.bfloat16)
            return running + jnp.dot(left_env[term_id, block_id], half, preferred_element_type=jnp.float32), None

        running, unused = lax.scan(per_term, jnp.zeros((W, W), jnp.float32), jnp.arange(TERMS, dtype=jnp.int32))
        return jnp.where(keep[block_id], running, jnp.zeros_like(running)).astype(jnp.bfloat16)

    result = lax.map(per_block, jnp.arange(NBLK, dtype=jnp.int32))
    return result.reshape(NBLK * W, W)
```

```python
import functools

import jax
import jax.numpy as jnp
from jax import lax
from jax.experimental import pallas as pl
from jax.experimental.pallas import tpu as pltpu
from jax.sharding import PartitionSpec as P

MESH = pl.DeviceIdType.MESH
BF = jnp.bfloat16
F32 = jnp.float32
GROUP = 6


def keep_mask(dims, block, first_row, shape):
    rows = lax.broadcasted_iota(jnp.int32, shape, 0) + first_row
    cols = lax.broadcasted_iota(jnp.int32, shape, 1)
    return (rows < dims[0, block]) & (cols < dims[1, block])


def kernel(
    src, dims, psi, left, right, out,
    lv, rv, blocks, wide, acc, parts, got,
    env_sem, line_send, line_recv, plane_send, plane_recv, side_send, side_recv, sum_send, sum_recv,
):
    s, o = lax.axis_index("sec"), lax.axis_index("op")
    y, z = lax.div(o, 4), lax.rem(o, 4)
    terms = lv.shape[1]
    groups = terms // GROUP
    side = psi.shape[1]

    def env_copies(i, g):
        k = lax.rem(y + 1 + i, 4)
        span = pl.ds(g * GROUP, GROUP)
        return (
            pltpu.make_async_copy(left.at[span, k], lv.at[i, span], env_sem.at[0, i, g]),
            pltpu.make_async_copy(right.at[span, k], rv.at[i, span], env_sem.at[1, i, g]),
        )

    @pl.loop(0, 4)
    def _(i):
        @pl.loop(0, groups)
        def _(g):
            for copy in env_copies(i, g):
                copy.start()

    def at(row, col):
        return {"op": row * 4 + col}

    barrier = pltpu.get_barrier_semaphore()
    for d in range(1, 4):
        pl.semaphore_signal(barrier, inc=1, device_id=at(y, lax.rem(z + d, 4)), device_id_type=MESH)
        pl.semaphore_signal(barrier, inc=1, device_id=at(lax.rem(y + d, 4), z), device_id_type=MESH)

    @pl.when(s > 0)
    def _():
        pl.semaphore_signal(barrier, inc=1, device_id={"sec": s - 1}, device_id_type=MESH)

    @pl.when(s < 7)
    def _():
        pl.semaphore_signal(barrier, inc=1, device_id={"sec": s + 1}, device_id_type=MESH)

    keep = keep_mask(dims, 4 * s + y, z * 64, psi.shape)
    mine = jnp.where(keep, psi[...], jnp.zeros_like(psi))
    blocks[2 + y, z] = mine.reshape(2, 32, side)
    got[o] = jnp.zeros_like(psi)

    pl.semaphore_wait(barrier, 6 + jnp.where(s > 0, 1, 0) + jnp.where(s < 7, 1, 0))

    def send(ref, dst, send_sem, recv_sem, device):
        return pltpu.make_async_remote_copy(
            src_ref=ref, dst_ref=dst, send_sem=send_sem, recv_sem=recv_sem,
            device_id=device, device_id_type=MESH,
        )

    def line(d, h):
        ref = blocks.at[2 + y, z, h]
        device = at(y, lax.rem(z + d, 4)) if h == 0 else at(lax.rem(y + d, 4), z)
        return send(ref, ref, line_send.at[h, d - 1], line_recv.at[h], device)

    def plane(d, h):
        if h == 0:
            ref = blocks.at[2 + y, :, 0]
            device = at(lax.rem(y + d, 4), z)
        else:
            ref = blocks.at[2:6, z, 1]
            device = at(y, lax.rem(z + d, 4))
        return send(ref, ref, plane_send.at[h, d - 1], plane_recv.at[h, d - 1], device)

    def up_row(row):
        return row >= 2

    def side_row(d, action):
        row = lax.rem(y + 4 - d, 4)

        @pl.when((row >= 2) & (s < 7))
        def _():
            copy = send(
                blocks.at[2 + row, :, 0], blocks.at[row - 2, :, 0],
                side_send.at[0, d], side_recv.at[0], {"sec": s + 1},
            )
            action(copy)

        @pl.when((row < 2) & (s > 0))
        def _():
            copy = send(
                blocks.at[2 + row, :, 0], blocks.at[6 + row, :, 0],
                side_send.at[0, d], side_recv.at[1], {"sec": s - 1},
            )
            action(copy)

    def side_col(d, action):
        col = lax.rem(z + 4 - d, 4)

        @pl.when(s < 7)
        def _():
            copy = send(
                blocks.at[4:6, col, 1], blocks.at[0:2, col, 1],
                side_send.at[1, d], side_recv.at[0], {"sec": s + 1},
            )
            action(copy)

        @pl.when(s > 0)
        def _():
            copy = send(
                blocks.at[2:4, col, 1], blocks.at[6:8, col, 1],
                side_send.at[2, d], side_recv.at[1], {"sec": s - 1},
            )
            action(copy)

    start = lambda copy: copy.start()
    wait_send = lambda copy: copy.wait_send()

    for d in range(1, 4):
        line(d, 0).start()
        line(d, 1).start()

    def wait_bytes(ref, sem):
        pltpu.make_async_copy(ref, ref, sem).wait()

    wait_bytes(blocks.at[2, 0:3, 0], line_recv.at[0])
    for d in range(1, 4):
        plane(d, 0).start()
    side_row(0, start)
    wait_bytes(blocks.at[2, 0:3, 1], line_recv.at[1])
    for d in range(1, 4):
        plane(d, 1).start()
    side_col(0, start)
    for d in range(1, 4):
        plane(d, 0).wait_recv()
        side_row(d, start)
        plane(d, 1).wait_recv()
        side_col(d, start)

    @pl.when(s > 0)
    def _():
        wait_bytes(blocks.at[0:2], side_recv.at[0])

    @pl.when(s < 7)
    def _():
        wait_bytes(blocks.at[6:8], side_recv.at[1])

    base = 4 * s - 2

    def sum_copy(i, q):
        k = lax.rem(y + 1 + i, 4)
        return send(
            parts.at[i, q], got.at[o], sum_send.at[i, q], sum_recv.at[0], at(k, q)
        )

    @pl.loop(0, 4)
    def _(i):
        k = lax.rem(y + 1 + i, 4)
        acc[...] = jnp.zeros_like(acc)

        @pl.loop(0, groups)
        def _(g):
            for copy in env_copies(i, g):
                copy.wait()
            t0 = g * GROUP
            for u in range(GROUP):
                block = blocks[jnp.clip(src[k, t0 + u] - base, 0, 7)].reshape(side, side)
                wide[:, u * side : (u + 1) * side] = jnp.dot(
                    lv[i, t0 + u], block, preferred_element_type=F32
                ).astype(BF)
            tall = rv[i, pl.ds(t0, GROUP)].reshape(GROUP * side, side)
            acc[...] += jnp.dot(wide[...], tall, preferred_element_type=F32)

        parts[i] = acc[...].astype(BF).reshape(4, 64, side)
        for q in range(4):
            @pl.when((i < 3) | (q != z))
            def _():
                sum_copy(i, q).start()

    total = acc[pl.ds(pl.multiple_of(z * 64, 64), 64), :]
    wait_bytes(got.at[0:15], sum_recv.at[0])
    for j in range(16):
        total = total + got[j].astype(F32)
    out[...] = jnp.where(keep, total, jnp.zeros_like(total)).astype(BF)

    for d in range(1, 4):
        for h in range(2):
            line(d, h).wait_send()
            plane(d, h).wait_send()
    for d in range(4):
        side_row(d, wait_send)
        side_col(d, wait_send)
    for i in range(4):
        for q in range(4):
            @pl.when((i < 3) | (q != z))
            def _():
                sum_copy(i, q).wait_send()


def shards(psi, left_env, right_env, term_src, block_dims):
    terms, per_sec, side, _ = left_env.shape
    dma = pltpu.SemaphoreType.DMA
    vmem = pl.BlockSpec(memory_space=pltpu.VMEM)
    smem = pl.BlockSpec(memory_space=pltpu.SMEM)
    hbm = pl.BlockSpec(memory_space=pl.ANY)
    return pl.pallas_call(
        kernel,
        out_shape=jax.ShapeDtypeStruct(psi.shape, BF),
        in_specs=[smem, smem, vmem, hbm, hbm],
        out_specs=vmem,
        scratch_shapes=[
            pltpu.VMEM((per_sec, terms, side, side), BF),
            pltpu.VMEM((per_sec, terms, side, side), BF),
            pltpu.VMEM((8, 4, 2, 32, side), BF),
            pltpu.VMEM((side, GROUP * side), BF),
            pltpu.VMEM((side, side), F32),
            pltpu.VMEM((4, 4, 64, side), BF),
            pltpu.VMEM((16, 64, side), BF),
            dma((2, 4, terms // GROUP)),
            dma((2, 3)),
            dma((2,)),
            dma((2, 3)),
            dma((2, 3)),
            dma((3, 4)),
            dma((2,)),
            dma((4, 4)),
            dma((1,)),
        ],
        compiler_params=pltpu.CompilerParams(
            collective_id=0, has_side_effects=True, vmem_limit_bytes=48 * 2**20
        ),
    )(term_src.T, block_dims, psi, left_env, right_env)


def solution(mesh):
    placed = (
        P(("sec", "op"), None),
        P("op", "sec", None, None),
        P("op", "sec", None, None),
        P("op", "sec"),
        P(),
    )
    return jax.shard_map(
        shards, mesh=mesh, in_specs=placed, out_specs=P(("sec", "op"), None), check_vma=False
    )
```

```python
import jax
import jax.numpy as jnp
from jax import lax
from jax.experimental import pallas as pl
from jax.experimental.pallas import tpu as pltpu
from jax.sharding import PartitionSpec as P

MESH = pl.DeviceIdType.MESH
BF = jnp.bfloat16
F32 = jnp.float32
GROUP = 6
OFFSETS = sorted(
    [(a, b) for a in range(4) for b in range(4) if a or b],
    key=lambda p: min(p[0], 4 - p[0]) + min(p[1], 4 - p[1]),
)


def keep_mask(dims, block, first_row, shape):
    rows = lax.broadcasted_iota(jnp.int32, shape, 0) + first_row
    cols = lax.broadcasted_iota(jnp.int32, shape, 1)
    return (rows < dims[0, block]) & (cols < dims[1, block])


def kernel(
    src_hbm, dims_hbm, psi_hbm, left, right, out,
    src, dims, psi, lv, rv, blocks, across, wide, acc, parts, got,
    small_sem, env_sem, plane_send, plane_recv, side_send, chip_recv, across_recv, sum_send, sum_recv,
):
    s, o = lax.axis_index("sec"), lax.axis_index("op")
    y, z = lax.div(o, 4), lax.rem(o, 4)
    core = lax.rem(s, 2)
    terms = lv.shape[1]
    groups = terms // GROUP
    side = psi.shape[1]

    small = [
        pltpu.make_async_copy(psi_hbm, psi, small_sem.at[0]),
        pltpu.make_async_copy(dims_hbm, dims, small_sem.at[1]),
        pltpu.make_async_copy(src_hbm, src, small_sem.at[2]),
    ]
    for copy in small:
        copy.start()

    odd = lax.rem(y, 2)
    first = 2 - 2 * core
    last = 2 * core
    order = [first + odd, first + 1 - odd, last + 1 - odd, last + odd]

    def env_copies(i, g):
        span = pl.ds(g * GROUP, GROUP)
        return (
            pltpu.make_async_copy(left.at[span, order[i]], lv.at[i, span], env_sem.at[0, i, g]),
            pltpu.make_async_copy(right.at[span, order[i]], rv.at[i, span], env_sem.at[1, i, g]),
        )

    def peer(d):
        return {"op": lax.rem(y + OFFSETS[d][0], 4) * 4 + lax.rem(z + OFFSETS[d][1], 4)}

    barrier = pltpu.get_barrier_semaphore()
    for d in range(15):
        pl.semaphore_signal(barrier, inc=1, device_id=peer(d), device_id_type=MESH)

    @pl.when(s > 0)
    def _():
        pl.semaphore_signal(barrier, inc=1, device_id={"sec": s - 1}, device_id_type=MESH)

    @pl.when(s < 7)
    def _():
        pl.semaphore_signal(barrier, inc=1, device_id={"sec": s + 1}, device_id_type=MESH)

    for i in range(4):
        for g in range(groups):
            for copy in env_copies(i, g):
                copy.start()

    small[0].wait()
    small[1].wait()
    keep = keep_mask(dims, 4 * s + y, z * 64, psi.shape)
    mine = psi[...]
    blocks[2 + y, z] = jnp.where(keep, mine, jnp.zeros_like(mine))
    got[o] = jnp.zeros_like(mine)

    pl.semaphore_wait(barrier, 15 + jnp.where(s > 0, 1, 0) + jnp.where(s < 7, 1, 0))

    def send(ref, dst, send_sem, recv_sem, device):
        return pltpu.make_async_remote_copy(
            src_ref=ref, dst_ref=dst, send_sem=send_sem, recv_sem=recv_sem,
            device_id=device, device_id_type=MESH,
        )

    def wait_bytes(ref, sem):
        pltpu.make_async_copy(ref, ref, sem).wait()

    def plane(d):
        ref = blocks.at[2 + y, z]
        return send(ref, ref, plane_send.at[d], plane_recv.at[d], peer(d))

    def forward(n, row, col, action):
        up = row >= 2
        to = s + jnp.where(up, 1, -1)
        on_chip = up == (core == 0)

        @pl.when(on_chip)
        def _():
            place = jnp.where(up, row - 2, row + 6)
            action(
                send(blocks.at[2 + row, col], blocks.at[place, col], side_send.at[n], chip_recv.at[0], {"sec": to})
            )

        @pl.when(jnp.logical_not(on_chip) & (to >= 0) & (to <= 7))
        def _():
            action(
                send(
                    blocks.at[2 + row, col], across.at[lax.rem(row, 2), col],
                    side_send.at[n], across_recv.at[0], {"sec": to},
                )
            )

    def forward_from(d, action):
        row, col = OFFSETS[d]
        forward(d, lax.rem(y + 4 - row, 4), lax.rem(z + 4 - col, 4), action)

    start = lambda copy: copy.start()
    wait_send = lambda copy: copy.wait_send()

    forward(15, y, z, start)
    for d in range(15):
        plane(d).start()
    for d in range(15):
        plane(d).wait_recv()
        forward_from(d, start)
    wait_bytes(blocks.at[0:2], chip_recv.at[0])
    small[2].wait()
    for i in range(4):
        for g in range(groups):
            for copy in env_copies(i, g):
                copy.wait()

    base = 4 * s - 2

    def sum_copy(i, q):
        return send(parts.at[i, q], got.at[o], sum_send.at[i, q], sum_recv.at[0], {"op": 4 * order[i] + q})

    def each_sum(i, action):
        for q in range(4):
            if i in (1, 2):
                action(sum_copy(i, q))
            else:
                @pl.when(4 * order[i] + q != o)
                def _():
                    action(sum_copy(i, q))

    for i in range(4):
        k = order[i]
        if i == 2:
            inside = jnp.where(core == 0, s > 0, s < 7)

            @pl.when(inside)
            def _():
                wait_bytes(across, across_recv.at[0])
                blocks[pl.ds(6 * core, 2)] = across[...]

        for g in range(groups):
            t0 = g * GROUP
            for u in range(GROUP):
                block = blocks[jnp.clip(src[k, t0 + u] - base, 0, 7)].reshape(side, side)
                wide[g % 2, :, u * side : (u + 1) * side] = jnp.dot(
                    lv[i, t0 + u], block, preferred_element_type=F32
                ).astype(BF)
            tall = rv[i, t0 : t0 + GROUP].reshape(GROUP * side, side)
            part = jnp.dot(wide[g % 2], tall, preferred_element_type=F32)
            if g == 0:
                acc[i] = part
            else:
                acc[i] += part

        parts[i] = acc[i].astype(BF).reshape(4, 64, side)
        each_sum(i, start)

    own = jnp.where((y >= 2) == (core == 1), 3, 0)
    total = acc[own, pl.ds(pl.multiple_of(z * 64, 64), 64), :]
    wait_bytes(got.at[0:15], sum_recv.at[0])
    for j in range(16):
        total = total + got[j].astype(F32)
    out[...] = jnp.where(keep, total, jnp.zeros_like(total)).astype(BF)

    for d in range(15):
        plane(d).wait_send()
        forward_from(d, wait_send)
    forward(15, y, z, wait_send)
    for i in range(4):
        each_sum(i, wait_send)


def shards(psi, left_env, right_env, term_src, block_dims):
    terms, per_sec, side, _ = left_env.shape
    rows = psi.shape[0]
    dma = pltpu.SemaphoreType.DMA
    return pl.pallas_call(
        kernel,
        out_shape=jax.ShapeDtypeStruct(psi.shape, BF),
        in_specs=[pl.BlockSpec(memory_space=pl.ANY)] * 5,
        out_specs=pl.BlockSpec(memory_space=pltpu.VMEM),
        scratch_shapes=[
            pltpu.SMEM((per_sec, terms), jnp.int32),
            pltpu.SMEM(block_dims.shape, jnp.int32),
            pltpu.VMEM(psi.shape, BF),
            pltpu.VMEM((per_sec, terms, side, side), BF),
            pltpu.VMEM((per_sec, terms, side, side), BF),
            pltpu.VMEM((8, 4, rows, side), BF),
            pltpu.VMEM((2, 4, rows, side), BF),
            pltpu.VMEM((2, side, GROUP * side), BF),
            pltpu.VMEM((4, side, side), F32),
            pltpu.VMEM((4, 4, rows, side), BF),
            pltpu.VMEM((16, rows, side), BF),
            dma((3,)),
            dma((2, 4, terms // GROUP)),
            dma((15,)),
            dma((15,)),
            dma((16,)),
            dma((1,)),
            dma((1,)),
            dma((4, 4)),
            dma((1,)),
        ],
        compiler_params=pltpu.CompilerParams(
            collective_id=0, has_side_effects=True, vmem_limit_bytes=48 * 2**20
        ),
    )(*[pltpu.with_memory_space_constraint(a, pltpu.HBM) for a in (term_src.T, block_dims, psi, left_env, right_env)])


def solution(mesh):
    placed = (
        P(("sec", "op"), None),
        P("op", "sec", None, None),
        P("op", "sec", None, None),
        P("op", "sec"),
        P(),
    )
    return jax.shard_map(
        shards, mesh=mesh, in_specs=placed, out_specs=P(("sec", "op"), None), check_vma=False
    )
```

```python
import jax
import jax.numpy as jnp
from jax import lax
from jax.experimental import pallas as pl
from jax.experimental.pallas import tpu as pltpu
from jax.sharding import PartitionSpec as P

MESH = pl.DeviceIdType.MESH
BF = jnp.bfloat16
F32 = jnp.float32
GROUP = 6
OFFSETS = sorted(
    [(a, b) for a in range(4) for b in range(4) if a or b],
    key=lambda p: (min(p[0], 4 - p[0]) + min(p[1], 4 - p[1]), p[1] != 0),
)


def keep_mask(dims, block, first_row, shape):
    rows = lax.broadcasted_iota(jnp.int32, shape, 0) + first_row
    cols = lax.broadcasted_iota(jnp.int32, shape, 1)
    return (rows < dims[0, block]) & (cols < dims[1, block])


def kernel(
    src_hbm, dims_hbm, psi_hbm, left, right, out,
    src, dims, psi, lv, rv, blocks, across, wide, acc, parts, got,
    small_sem, env_sem, plane_send, plane_recv, side_send, chip_recv, across_recv, sum_send, sum_recv,
):
    s, o = lax.axis_index("sec"), lax.axis_index("op")
    y, z = lax.div(o, 4), lax.rem(o, 4)
    core = lax.rem(s, 2)
    terms = lv.shape[1]
    groups = terms // GROUP
    side = psi.shape[1]

    small = [
        pltpu.make_async_copy(psi_hbm, psi, small_sem.at[0]),
        pltpu.make_async_copy(dims_hbm, dims, small_sem.at[1]),
        pltpu.make_async_copy(src_hbm, src, small_sem.at[2]),
    ]
    for copy in small:
        copy.start()

    odd = lax.rem(y, 2)
    near = 2 - 2 * core
    far = 2 * core
    end = jnp.where((y >= 2) == (core == 1), y, 3 - y)
    order = [near + odd, near + 1 - odd, 4 * core + 1 - end, end]

    def env_copies(i):
        return (
            pltpu.make_async_copy(left.at[:, order[i]], lv.at[i], env_sem.at[0, i]),
            pltpu.make_async_copy(right.at[:, order[i]], rv.at[i], env_sem.at[1, i]),
        )

    def peer(d):
        return {"op": lax.rem(y + OFFSETS[d][0], 4) * 4 + lax.rem(z + OFFSETS[d][1], 4)}

    barrier = pltpu.get_barrier_semaphore()
    for d in reversed(range(15)):
        pl.semaphore_signal(barrier, inc=1, device_id=peer(d), device_id_type=MESH)

    @pl.when(s > 0)
    def _():
        pl.semaphore_signal(barrier, inc=1, device_id={"sec": s - 1}, device_id_type=MESH)

    @pl.when(s < 7)
    def _():
        pl.semaphore_signal(barrier, inc=1, device_id={"sec": s + 1}, device_id_type=MESH)

    small[0].wait()
    small[1].wait()
    keep = keep_mask(dims, 4 * s + y, z * 64, psi.shape)
    mine = psi[...]
    blocks[2 + y, z] = jnp.where(keep, mine, jnp.zeros_like(mine))
    got[o] = jnp.zeros_like(mine)

    pl.semaphore_wait(barrier, 15 + jnp.where(s > 0, 1, 0) + jnp.where(s < 7, 1, 0))

    def send(ref, dst, send_sem, recv_sem, device):
        return pltpu.make_async_remote_copy(
            src_ref=ref, dst_ref=dst, send_sem=send_sem, recv_sem=recv_sem,
            device_id=device, device_id_type=MESH,
        )

    def wait_bytes(ref, sem):
        pltpu.make_async_copy(ref, ref, sem).wait()

    def plane(d):
        ref = blocks.at[2 + y, z]
        return send(ref, ref, plane_send.at[d], plane_recv.at[o], peer(d))

    def arrived(row, col):
        wait_bytes(blocks.at[2 + row, col], plane_recv.at[4 * row + col])

    waits = (y >= 2) == (core == 1)
    sibling = s + 1 - 2 * core
    beyond = s - 1 + 2 * core

    def slabs(pair):
        return [(pair + a, lax.rem(z + b, 4), 4 * a + b) for a in range(2) for b in range(4)]

    def to_sibling(row, col, n, action):
        place = row - 2 + 8 * core
        action(send(blocks.at[2 + row, col], blocks.at[place, col], side_send.at[n], chip_recv.at[0], {"sec": sibling}))

    def to_beyond(row, col, n, action):
        @pl.when((beyond >= 0) & (beyond <= 7))
        def _():
            action(
                send(
                    blocks.at[2 + row, col], across.at[lax.rem(row, 2), col],
                    side_send.at[8 + n], across_recv.at[0], {"sec": beyond},
                )
            )

    start = lambda copy: copy.start()
    wait_send = lambda copy: copy.wait_send()

    for d in reversed(range(15)):
        plane(d).start()
    for i in range(4):
        for copy in env_copies(i):
            copy.start()
    for row, col, n in slabs(near):
        @pl.when(((row != y) | (col != z)))
        def _():
            arrived(row, col)
        to_sibling(row, col, n, start)
    for row, col, n in slabs(far):
        @pl.when((row != y) | (col != z))
        def _():
            arrived(row, col)
        to_beyond(row, col, n, start)
    wait_bytes(blocks.at[0:2], chip_recv.at[0])
    small[2].wait()
    for i in range(4):
        for copy in env_copies(i):
            copy.wait()

    base = 4 * s - 2

    def sum_copy(i, q):
        return send(parts.at[i, q], got.at[o], sum_send.at[i, q], sum_recv.at[0], {"op": 4 * order[i] + q})

    def each_sum(i, quarters, action):
        for q in quarters:
            if i in (1, 2):
                action(sum_copy(i, q))
            else:
                @pl.when(4 * order[i] + q != o)
                def _():
                    action(sum_copy(i, q))

    for i in range(4):
        k = order[i]
        if i == 2:
            inside = jnp.where(core == 0, s > 0, s < 7)

            @pl.when(inside)
            def _():
                wait_bytes(across, across_recv.at[0])
                blocks[pl.ds(6 * core, 2)] = across[...]

        for lo, hi in ((0, side),) if i < 3 else ((0, side // 2), (side // 2, side)):
            for g in range(groups):
                t0 = g * GROUP
                for u in range(GROUP):
                    block = blocks[jnp.clip(src[k, t0 + u] - base, 0, 7)].reshape(side, side)
                    wide[g % 2, lo:hi, u * side : (u + 1) * side] = jnp.dot(
                        lv[i, t0 + u, lo:hi], block, preferred_element_type=F32
                    ).astype(BF)
                tall = rv[i, t0 : t0 + GROUP].reshape(GROUP * side, side)
                part = jnp.dot(wide[g % 2, lo:hi], tall, preferred_element_type=F32)
                if g == 0:
                    acc[i, lo:hi] = part
                else:
                    acc[i, lo:hi] += part

            parts[i, lo // 64 : hi // 64] = acc[i, lo:hi].astype(BF).reshape((hi - lo) // 64, 64, side)
            each_sum(i, range(lo // 64, hi // 64), start)

    for d in range(15):
        plane(d).wait_send()
    for row, col, n in slabs(near):
        to_sibling(row, col, n, wait_send)
    for row, col, n in slabs(far):
        to_beyond(row, col, n, wait_send)
    for i in range(4):
        each_sum(i, range(4), wait_send)

    own = jnp.where((y >= 2) == (core == 1), 3, 0)
    total = acc[own, pl.ds(pl.multiple_of(z * 64, 64), 64), :]
    wait_bytes(got.at[0:15], sum_recv.at[0])
    for j in range(16):
        total = total + got[j].astype(F32)
    out[...] = jnp.where(keep, total, jnp.zeros_like(total)).astype(BF)


def shards(psi, left_env, right_env, term_src, block_dims):
    terms, per_sec, side, _ = left_env.shape
    rows = psi.shape[0]
    dma = pltpu.SemaphoreType.DMA
    return pl.pallas_call(
        kernel,
        out_shape=jax.ShapeDtypeStruct(psi.shape, BF),
        in_specs=[pl.BlockSpec(memory_space=pl.ANY)] * 5,
        out_specs=pl.BlockSpec(memory_space=pltpu.VMEM),
        scratch_shapes=[
            pltpu.SMEM((per_sec, terms), jnp.int32),
            pltpu.SMEM(block_dims.shape, jnp.int32),
            pltpu.VMEM(psi.shape, BF),
            pltpu.VMEM((per_sec, terms, side, side), BF),
            pltpu.VMEM((per_sec, terms, side, side), BF),
            pltpu.VMEM((8, 4, rows, side), BF),
            pltpu.VMEM((2, 4, rows, side), BF),
            pltpu.VMEM((2, side, GROUP * side), BF),
            pltpu.VMEM((4, side, side), F32),
            pltpu.VMEM((4, 4, rows, side), BF),
            pltpu.VMEM((16, rows, side), BF),
            dma((3,)),
            dma((2, 4)),
            dma((15,)),
            dma((16,)),
            dma((16,)),
            dma((1,)),
            dma((1,)),
            dma((4, 4)),
            dma((1,)),
        ],
        compiler_params=pltpu.CompilerParams(
            collective_id=0, has_side_effects=True, vmem_limit_bytes=48 * 2**20
        ),
    )(*[pltpu.with_memory_space_constraint(a, pltpu.HBM) for a in (term_src.T, block_dims, psi, left_env, right_env)])


def solution(mesh):
    placed = (
        P(("sec", "op"), None),
        P("op", "sec", None, None),
        P("op", "sec", None, None),
        P("op", "sec"),
        P(),
    )
    return jax.shard_map(
        shards, mesh=mesh, in_specs=placed, out_specs=P(("sec", "op"), None), check_vma=False
    )
```

```python
import jax
import jax.numpy as jnp
from jax import lax
from jax.experimental import pallas as pl
from jax.experimental.pallas import tpu as pltpu
from jax.sharding import PartitionSpec as P

MESH = pl.DeviceIdType.MESH
BF = jnp.bfloat16
F32 = jnp.float32
GROUP = 6
OFFSETS = sorted(
    [(a, b) for a in range(4) for b in range(4) if a or b],
    key=lambda p: (min(p[0], 4 - p[0]) + min(p[1], 4 - p[1]), p[1] != 0),
)


def keep_mask(dims, block, first_row, shape):
    rows = lax.broadcasted_iota(jnp.int32, shape, 0) + first_row
    cols = lax.broadcasted_iota(jnp.int32, shape, 1)
    return (rows < dims[0, block]) & (cols < dims[1, block])


def kernel(
    src_hbm, dims_hbm, psi_hbm, left, right, out,
    src, dims, psi, lv, rv, blocks, across, wide, acc, parts, got,
    small_sem, env_sem, plane_send, plane_recv, side_send, chip_recv, across_recv, sum_send, sum_recv,
):
    s, o = lax.axis_index("sec"), lax.axis_index("op")
    y, z = lax.div(o, 4), lax.rem(o, 4)
    core = lax.rem(s, 2)
    terms = lv.shape[1]
    groups = terms // GROUP
    side = psi.shape[1]

    small = [
        pltpu.make_async_copy(psi_hbm, psi, small_sem.at[0]),
        pltpu.make_async_copy(dims_hbm, dims, small_sem.at[1]),
        pltpu.make_async_copy(src_hbm, src, small_sem.at[2]),
    ]
    for copy in small:
        copy.start()

    odd = lax.rem(y, 2)
    near = 2 - 2 * core
    far = 2 * core
    end = jnp.where((y >= 2) == (core == 1), y, 3 - y)
    order = [near + odd, near + 1 - odd, 4 * core + 1 - end, end]

    def env_copies(i):
        return (
            pltpu.make_async_copy(left.at[:, order[i]], lv.at[i], env_sem.at[0, i]),
            pltpu.make_async_copy(right.at[:, order[i]], rv.at[i], env_sem.at[1, i]),
        )

    def peer(d):
        return {"op": lax.rem(y + OFFSETS[d][0], 4) * 4 + lax.rem(z + OFFSETS[d][1], 4)}

    barrier = pltpu.get_barrier_semaphore()
    for d in reversed(range(15)):
        pl.semaphore_signal(barrier, inc=1, device_id=peer(d), device_id_type=MESH)

    @pl.when(s > 0)
    def _():
        pl.semaphore_signal(barrier, inc=1, device_id={"sec": s - 1}, device_id_type=MESH)

    @pl.when(s < 7)
    def _():
        pl.semaphore_signal(barrier, inc=1, device_id={"sec": s + 1}, device_id_type=MESH)

    small[0].wait()
    small[1].wait()
    keep = keep_mask(dims, 4 * s + y, z * 64, psi.shape)
    mine = psi[...]
    blocks[2 + y, z] = jnp.where(keep, mine, jnp.zeros_like(mine))
    got[o] = jnp.zeros_like(mine)

    for i in range(4):
        for copy in env_copies(i):
            copy.start()
    pl.semaphore_wait(barrier, 15 + jnp.where(s > 0, 1, 0) + jnp.where(s < 7, 1, 0))

    def send(ref, dst, send_sem, recv_sem, device):
        return pltpu.make_async_remote_copy(
            src_ref=ref, dst_ref=dst, send_sem=send_sem, recv_sem=recv_sem,
            device_id=device, device_id_type=MESH,
        )

    def wait_bytes(ref, sem):
        pltpu.make_async_copy(ref, ref, sem).wait()

    def plane(d):
        ref = blocks.at[2 + y, z]
        return send(ref, ref, plane_send.at[d], plane_recv.at[o], peer(d))

    def arrived(row, col):
        wait_bytes(blocks.at[2 + row, col], plane_recv.at[4 * row + col])

    waits = (y >= 2) == (core == 1)
    sibling = s + 1 - 2 * core
    beyond = s - 1 + 2 * core

    def slabs(pair):
        return [(pair + a, lax.rem(z + b, 4), 4 * a + b) for a in range(2) for b in range(4)]

    def to_sibling(row, col, n, action):
        place = row - 2 + 8 * core
        action(send(blocks.at[2 + row, col], blocks.at[place, col], side_send.at[n], chip_recv.at[0], {"sec": sibling}))

    def to_beyond(row, col, n, action):
        @pl.when((beyond >= 0) & (beyond <= 7))
        def _():
            action(
                send(
                    blocks.at[2 + row, col], across.at[lax.rem(row, 2), col],
                    side_send.at[8 + n], across_recv.at[0], {"sec": beyond},
                )
            )

    start = lambda copy: copy.start()
    wait_send = lambda copy: copy.wait_send()

    for d in reversed(range(15)):
        plane(d).start()
    for row, col, n in slabs(near):
        @pl.when(((row != y) | (col != z)))
        def _():
            arrived(row, col)
        to_sibling(row, col, n, start)
    for row, col, n in slabs(far):
        @pl.when((row != y) | (col != z))
        def _():
            arrived(row, col)
        to_beyond(row, col, n, start)
    wait_bytes(blocks.at[0:2], chip_recv.at[0])
    small[2].wait()
    for i in range(4):
        for copy in env_copies(i):
            copy.wait()

    base = 4 * s - 2

    def sum_copy(i, q):
        return send(parts.at[i, q], got.at[o], sum_send.at[i, q], sum_recv.at[0], {"op": 4 * order[i] + q})

    def each_sum(i, quarters, action):
        for q in quarters:
            if i in (1, 2):
                action(sum_copy(i, q))
            else:
                @pl.when(4 * order[i] + q != o)
                def _():
                    action(sum_copy(i, q))

    for i in range(4):
        k = order[i]
        if i == 2:
            inside = jnp.where(core == 0, s > 0, s < 7)

            @pl.when(inside)
            def _():
                wait_bytes(across, across_recv.at[0])
                blocks[pl.ds(6 * core, 2)] = across[...]

        for lo, hi in ((0, side),) if i < 3 else ((0, side // 2), (side // 2, side)):
            for g in range(groups):
                t0 = g * GROUP
                for u in range(GROUP):
                    block = blocks[jnp.clip(src[k, t0 + u] - base, 0, 7)].reshape(side, side)
                    wide[g % 2, lo:hi, u * side : (u + 1) * side] = jnp.dot(
                        lv[i, t0 + u, lo:hi], block, preferred_element_type=F32
                    ).astype(BF)
                tall = rv[i, t0 : t0 + GROUP].reshape(GROUP * side, side)
                part = jnp.dot(wide[g % 2, lo:hi], tall, preferred_element_type=F32)
                if g == 0:
                    acc[i, lo:hi] = part
                else:
                    acc[i, lo:hi] += part

            parts[i, lo // 64 : hi // 64] = acc[i, lo:hi].astype(BF).reshape((hi - lo) // 64, 64, side)
            each_sum(i, range(lo // 64, hi // 64), start)

    for d in range(15):
        plane(d).wait_send()
    for row, col, n in slabs(near):
        to_sibling(row, col, n, wait_send)
    for row, col, n in slabs(far):
        to_beyond(row, col, n, wait_send)
    for i in range(4):
        each_sum(i, range(4), wait_send)

    own = jnp.where((y >= 2) == (core == 1), 3, 0)
    total = acc[own, pl.ds(pl.multiple_of(z * 64, 64), 64), :]
    wait_bytes(got.at[0:15], sum_recv.at[0])
    for j in range(16):
        total = total + got[j].astype(F32)
    out[...] = jnp.where(keep, total, jnp.zeros_like(total)).astype(BF)


def shards(psi, left_env, right_env, term_src, block_dims):
    terms, per_sec, side, _ = left_env.shape
    rows = psi.shape[0]
    dma = pltpu.SemaphoreType.DMA
    return pl.pallas_call(
        kernel,
        out_shape=jax.ShapeDtypeStruct(psi.shape, BF),
        in_specs=[pl.BlockSpec(memory_space=pl.ANY)] * 5,
        out_specs=pl.BlockSpec(memory_space=pltpu.VMEM),
        scratch_shapes=[
            pltpu.SMEM((per_sec, terms), jnp.int32),
            pltpu.SMEM(block_dims.shape, jnp.int32),
            pltpu.VMEM(psi.shape, BF),
            pltpu.VMEM((per_sec, terms, side, side), BF),
            pltpu.VMEM((per_sec, terms, side, side), BF),
            pltpu.VMEM((8, 4, rows, side), BF),
            pltpu.VMEM((2, 4, rows, side), BF),
            pltpu.VMEM((2, side, GROUP * side), BF),
            pltpu.VMEM((4, side, side), F32),
            pltpu.VMEM((4, 4, rows, side), BF),
            pltpu.VMEM((16, rows, side), BF),
            dma((3,)),
            dma((2, 4)),
            dma((15,)),
            dma((16,)),
            dma((16,)),
            dma((1,)),
            dma((1,)),
            dma((4, 4)),
            dma((1,)),
        ],
        compiler_params=pltpu.CompilerParams(
            collective_id=0, has_side_effects=True, vmem_limit_bytes=48 * 2**20
        ),
    )(*[pltpu.with_memory_space_constraint(a, pltpu.HBM) for a in (term_src.T, block_dims, psi, left_env, right_env)])


def solution(mesh):
    placed = (
        P(("sec", "op"), None),
        P("op", "sec", None, None),
        P("op", "sec", None, None),
        P("op", "sec"),
        P(),
    )
    return jax.shard_map(
        shards, mesh=mesh, in_specs=placed, out_specs=P(("sec", "op"), None), check_vma=False
    )
```
